32 devices in a mesh: groups: 2 (over y), seq: 4 (over z), head: 2 (over x), sub: 2 (over core).
Axes of the slice: x: 2, y: 2, z: 4, core: 2. Of those that a mesh axis runs over, the one named last changes fastest.
Arguments:
- query: bfloat16 [8, 1024, 128], P('head', ('groups', 'seq')), parts along dimension 1, may hold values from -6 to 6
- key: bfloat16 [8, 1024, 128], P('head', ('groups', 'seq')), parts along dimension 1, may hold values from -6 to 6
- value: bfloat16 [8, 128, 1024], P('head', 'sub', ('groups', 'seq')), parts along dimension 2, may hold values from -6 to 6
- beta: float32 [8, 1024], P('head', ('groups', 'seq')), parts along dimension 1, may hold values from 0 to 0.98, as said below
- d_out: bfloat16 [8, 128, 1024], P('head', 'sub', ('groups', 'seq')), parts along dimension 2, may hold values from -6 to 6
Outputs:
- grad_query: float32 [8, 1024, 128], P('head', ('groups', 'seq')), parts along dimension 1
- grad_key: float32 [8, 1024, 128], P('head', ('groups', 'seq')), parts along dimension 1
- grad_value: float32 [8, 128, 1024], P('head', 'sub', ('groups', 'seq')), parts along dimension 2
- grad_beta: float32 [8, 1024], P('head', ('groups', 'seq')), parts along dimension 1
The draws below stay inside these ranges and needn't reach their ends.
There are 2 independent parts, one for each index of `groups`. The reference program is written for one: setup_inputs(seed, part) draws one part's arguments, and reference() takes and returns one part's arrays. A program takes and returns all parts, laid end to end along the dimension named above; each array names one. Nothing has to cross between parts.
Inputs may be any that keep to these rules, and one draw needn't show every extreme that they name: `beta`: every entry is positive.
All inputs are finite; a program needn't handle non-finite values.
Results may differ from the reference program's by a relative error of at most 0.0003.
Values may be sent and summed in bfloat16 or wider, within the bound.
A program may use at most 64 MiB of HBM per device.

```python
import math
import jax
import jax.numpy as jnp
from jax import lax

DK = 128
DV = 128
TOK_DEV = 128
HEADS = 8
SEQ = 512


def draw_beta(key, part):
    subkeys = jax.random.split(key, 6)
    fast_share = 0.5
    rough_low = 0.5
    rough_high = 1.5
    fast_heads = jax.random.uniform(subkeys[0], (HEADS, 1)) < fast_share
    slow_rate = DK / SEQ * jnp.exp(jax.random.uniform(subkeys[1], (HEADS, 1), minval=math.log(0.5), maxval=math.log(2.0)))
    fast_rate = jnp.exp(jax.random.uniform(subkeys[2], (HEADS, 1), minval=math.log(0.3), maxval=math.log(0.9)))
    base_rate = jnp.where(fast_heads, fast_rate, slow_rate)
    block_scale = jnp.exp(jax.random.uniform(subkeys[3], (HEADS, SEQ // TOK_DEV), minval=-math.log(2.0), maxval=math.log(2.0)))
    block_scale = jnp.repeat(block_scale, TOK_DEV, axis=1)
    rough = jax.random.uniform(subkeys[4], (HEADS, SEQ), minval=rough_low, maxval=rough_high)
    value_inputs = jnp.minimum(base_rate * block_scale * rough, 0.95)
    run_length = max(min(32, TOK_DEV // 4), 1)
    start_offsets = jax.random.randint(subkeys[5], (HEADS, 3, 1), 0, SEQ - run_length + 1)
    token_position = jnp.arange(SEQ)[None, None, :]
    write_spurt = jnp.any((token_position >= start_offsets) & (token_position < start_offsets + run_length), axis=1)
    return jnp.where(write_spurt, 0.98, value_inputs).astype(jnp.float32)


def steps_of(own_key, shape, cuts, low, largest):
    def one(dim, parts):
        steps = jax.random.uniform(jax.random.fold_in(jax.random.fold_in(own_key, 6), dim), (parts,), jnp.float32, low / len(cuts), largest / len(cuts))
        return jnp.repeat(jnp.exp(steps), shape[dim] // parts).reshape((-1,) + (1,) * (len(shape) - dim - 1))

    level = one(*cuts[0])
    for cut in cuts[1:]:
        level = level * one(*cut)
    return level


def scatter_about(rng, shape, deviation, bound, shards=(), kind=jnp.bfloat16):
    gain = steps_of(rng, shape, shards, -0.22, 0.18) if shards else 1.0
    drawn = jax.random.normal(rng, shape, jnp.float32) * deviation * gain
    return jnp.minimum(jnp.maximum(drawn, -bound), bound).astype(kind)


def setup_inputs(seed: int = 0, part: int = 0) -> dict:
    key_of = jax.random.split(jax.random.key(seed), 6)
    part_keys = jax.random.split(jax.random.fold_in(key_of[5], part), 6)
    query = scatter_about(part_keys[0], (HEADS, SEQ, DK), 1.0, 6.0, ((0, 2), (1, 4)))
    key = scatter_about(part_keys[1], (HEADS, SEQ, DK), 1.0, 6.0, ((0, 2), (1, 4)))
    value = scatter_about(part_keys[2], (HEADS, DV, SEQ), 1.0, 6.0, ((0, 2), (1, 2), (2, 4)))
    beta = draw_beta(jax.random.fold_in(jax.random.fold_in(key_of[5], part), 71), part)
    d_out = scatter_about(part_keys[4], (HEADS, DV, SEQ), 1.0, 6.0, ((0, 2), (1, 2), (2, 4)))
    return {"query": query, "key": key, "value": value, "beta": beta, "d_out": d_out}


EPS = 1e-06
HIGH = lax.Precision.HIGHEST

def token_step(memory_state, inputs):
    query_tok, key_tok, value_tok, beta_tok = inputs
    predicted = jnp.einsum('hvk,hk->hv', memory_state, key_tok, precision=HIGH)
    update = beta_tok[:, None] * (value_tok - predicted)
    memory_state = memory_state + update[:, :, None] * key_tok[:, None, :]
    output = jnp.einsum('hvk,hk->hv', memory_state, query_tok, precision=HIGH)
    return (memory_state, output)

@jax.checkpoint
def block_step(memory_state, inputs):
    return lax.scan(token_step, memory_state, inputs)

def loss_fn(query_f, key_f, value_f, beta_f, grad_out):
    unit_keys = key_f * lax.rsqrt(lax.optimization_barrier(jnp.sum(key_f * key_f, -1, keepdims=True)) + EPS)
    scaled = query_f * DK ** (-0.5)
    block_len = math.gcd(SEQ, 128)
    block_count = SEQ // block_len
    query_time = jnp.transpose(scaled, (1, 0, 2)).reshape(block_count, block_len, HEADS, DK)
    key_time = jnp.transpose(unit_keys, (1, 0, 2)).reshape(block_count, block_len, HEADS, DK)
    value_time = jnp.transpose(value_f, (2, 0, 1)).reshape(block_count, block_len, HEADS, DV)
    beta_time = jnp.transpose(beta_f, (1, 0)).reshape(block_count, block_len, HEADS)
    start = jnp.zeros((HEADS, DV, DK), jnp.float32)
    _, outputs = lax.scan(block_step, start, (query_time, key_time, value_time, beta_time))
    outputs = outputs.reshape(SEQ, HEADS, DV)
    return jnp.sum(outputs * jnp.transpose(grad_out, (2, 0, 1)))

def reference(query, key, value, beta, d_out):
    grads = jax.grad(loss_fn, argnums=(0, 1, 2, 3))(query.astype(jnp.float32), key.astype(jnp.float32), value.astype(jnp.float32), beta.astype(jnp.float32), d_out.astype(jnp.float32))
    return (grads[0], grads[1], grads[2], grads[3])
```

```python
import functools

import jax
import jax.numpy as jnp
from jax import lax
from jax.experimental import pallas as pl
from jax.experimental.pallas import tpu as pltpu
from jax.sharding import PartitionSpec as P

EPS = 1e-06
BASE = 16
F32 = jnp.float32
BF16 = jnp.bfloat16
MESH = pl.DeviceIdType.MESH


def split(x):
    hi = x.astype(BF16)
    return hi, (x - hi.astype(F32)).astype(BF16)


def nn(lhs, rhs):
    a = lhs[0] if len(lhs) == 1 else jnp.concatenate(lhs, axis=1)
    b = rhs[0] if len(rhs) == 1 else jnp.concatenate(rhs, axis=0)
    return jnp.dot(a, b, preferred_element_type=F32)


def nt(lhs, rhs):
    a = lhs[0] if len(lhs) == 1 else jnp.concatenate(lhs, axis=1)
    b = rhs[0] if len(rhs) == 1 else jnp.concatenate(rhs, axis=1)
    return lax.dot_general(a, b, (((1,), (1,)), ((), ())), preferred_element_type=F32)


def left3(s):
    return [s[0], s[0], s[1]]


def right3(s):
    return [s[0], s[1], s[0]]


def nn3(a, b):
    return nn(left3(a), right3(b))


def nt3(a, b):
    return nt(left3(a), right3(b))


def inverses(mats, row, col):
    size = mats[0].shape[0]
    heads = range(len(mats))
    eye = (row == col).astype(F32)
    near = (row // BASE) == (col // BASE)
    power = [split(jnp.where(near, -a, 0.0)) for a in mats]
    inv = [eye + jnp.where(near, -a, 0.0) for a in mats]
    reach = 2
    while reach < BASE:
        power = [split(nn3(p, p)) for p in power]
        inv = [inv[h] + nn3(split(inv[h]), power[h]) for h in heads]
        reach *= 2
    width = BASE
    while width < size:
        pair = ((row // (2 * width)) == (col // (2 * width))) & ((row // width) != (col // width))
        off = [split(jnp.where(pair, a, 0.0)) for a in mats]
        cut = [split(i) for i in inv]
        mid = [split(nn3(off[h], cut[h])) for h in heads]
        inv = [inv[h] - nn3(cut[h], mid[h]) for h in heads]
        width *= 2
    return inv


def kernel(
    n, q_ref, k_ref, v_ref, b_ref, g_ref, gq_ref, gk_ref, gv_ref, gb_ref,
    vin, gin, s_in, s_out, d_in, d_out, dt_s, xt_s, dm_s, gt_s, gvx, gbx,
    in_send, in_recv, f_send, f_recv, r_send, r_recv, o_send, o_recv,
):
    heads, toks, width = q_ref.shape
    mine = heads // 2
    half = v_ref.shape[1]
    idx = lax.axis_index("seq")
    sub = lax.axis_index("sub")
    other = 1 - sub
    right, left = lax.rem(idx + 1, n), lax.rem(idx + n - 1, n)
    scale = width ** (-0.5)
    base = sub * mine
    hs = range(mine)

    barrier = pltpu.get_barrier_semaphore()
    for target in ({"sub": other}, {"seq": right}, {"seq": left}):
        pl.semaphore_signal(barrier, inc=1, device_id=target, device_id_type=MESH)

    def remote(src, dst, send, recv, target):
        return pltpu.make_async_remote_copy(
            src_ref=src, dst_ref=dst, send_sem=send, recv_sem=recv,
            device_id=target, device_id_type=MESH,
        )

    away = pl.ds(other * mine, mine)
    v_copy = remote(v_ref.at[away], vin, in_send.at[0], in_recv.at[0], {"sub": other})
    g_copy = remote(g_ref.at[away], gin, in_send.at[1], in_recv.at[1], {"sub": other})

    def f_copy(h):
        return remote(s_out.at[h], s_in.at[h], f_send.at[h], f_recv.at[h], {"seq": right})

    def r_copy(h):
        return remote(d_out.at[h], d_in.at[h], r_send.at[h], r_recv.at[h], {"seq": left})

    def q_copy(h):
        at = gq_ref.at[base + h]
        return remote(at, at, o_send.at[0, h], o_recv.at[0, h], {"sub": other})

    def k_copy(h):
        at = gk_ref.at[base + h]
        return remote(at, at, o_send.at[1, h], o_recv.at[1, h], {"sub": other})

    def gv_copy(h):
        return remote(
            gvx.at[h], gv_ref.at[base + h], o_send.at[2, h], o_recv.at[2, h], {"sub": other}
        )

    gb_copy = remote(gbx.at[sub], gbx.at[sub], o_send.at[3, 0], o_recv.at[3, 0], {"sub": other})

    pl.semaphore_wait(barrier, 3)
    v_copy.start()
    g_copy.start()

    @pl.when(idx == 0)
    def _():
        s_in[...] = jnp.zeros_like(s_in)

    @pl.when(idx == n - 1)
    def _():
        d_in[...] = jnp.zeros_like(d_in)

    row = lax.broadcasted_iota(jnp.int32, (toks, toks), 0)
    col = lax.broadcasted_iota(jnp.int32, (toks, toks), 1)
    below, lower, above = row > col, row >= col, row < col
    eye = (row == col).astype(F32)

    kb = [k_ref[base + h] for h in hs]
    qb = [q_ref[base + h] for h in hs]
    kf = [k.astype(F32) for k in kb]
    r_col = [lax.rsqrt(jnp.sum(k * k, axis=1, keepdims=True) + EPS) for k in kf]
    r_row = [jnp.broadcast_to(r, (toks, toks)).T for r in r_col]
    b_row = [b_ref[pl.ds(base + h, 1), :] for h in hs]
    b_col = [jnp.broadcast_to(b, (toks, toks)).T for b in b_row]
    both = [nt([kb[h]], [kb[h]]) * r_col[h] * r_row[h] for h in hs]
    tri = inverses([jnp.where(below, b_col[h] * both[h], 0.0) for h in hs], row, col)
    kbt = [k.T for k in kb]
    tri_b = [split(tri[h] * b_row[h]) for h in hs]
    tri_br = [split(tri[h] * (b_row[h] * r_row[h])) for h in hs]
    w_t = [nt([kbt[h]] * 2, list(tri_br[h])) for h in hs]
    trans = [split(eye - nn(list(split(w_t[h] * r_row[h])), [kb[h]] * 2)) for h in hs]
    w_s = [split(w) for w in w_t]

    v_copy.wait_recv()
    g_copy.wait_recv()
    vt = [jnp.concatenate([v_ref[base + h], vin[h]], axis=0) for h in hs]
    gt = [jnp.concatenate([g_ref[base + h], gin[h]], axis=0) for h in hs]
    u_t = [nt([vt[h]] * 2, list(tri_b[h])) for h in hs]
    carry = [nn(list(split(u_t[h] * r_row[h])), [kb[h]] * 2) for h in hs]

    @pl.when(idx == 0)
    def _():
        for h in hs:
            s_out[h] = carry[h]
            f_copy(h).start()

    scores = [
        split(jnp.where(lower, nt([qb[h]], [kb[h]]) * (r_row[h] * scale), 0.0)) for h in hs
    ]
    dd0 = [split(nn([gt[h]] * 2, list(scores[h]))) for h in hs]
    tri_s = [split(t) for t in tri]
    g0 = [nn3(dd0[h], tri_s[h]) for h in hs]
    back = [
        nn([gt[h]], [qb[h]]) * scale
        - nn(list(split(g0[h] * (b_row[h] * r_row[h]))), [kb[h]] * 2)
        for h in hs
    ]

    @pl.when(idx == n - 1)
    def _():
        for h in hs:
            d_out[h] = back[h]
            r_copy(h).start()

    z_t = [
        split(nn([kbt[h]] * 2, list(split(tri[h] * r_col[h])))) for h in hs
    ]
    g_tok = [g.T for g in gt]

    def phase_f():
        for h in hs:

            @pl.when(idx > 0)
            def _():
                f_copy(h).wait_recv()

            @pl.when((idx > 0) & (idx < n - 1))
            def _():
                s_out[h] = nn3(split(s_in[h]), trans[h]) + carry[h]
                f_copy(h).start()

        for h in hs:
            state = split(s_in[h])
            d_t = u_t[h] - nn3(state, w_s[h])
            xt_s[h] = vt[h].astype(F32) - nt(list(state), [kb[h]] * 2) * r_row[h]
            dt_s[h] = d_t
            dm = jnp.where(lower, nn([g_tok[h]] * 2, list(split(d_t))), 0.0)
            dm_s[h] = dm.T * scale
            gq_ref[base + h] = scale * nn(
                [g_tok[h]] * 2 + list(split(dm * r_row[h])), list(state) + [kb[h]] * 2
            )
            q_copy(h).start()

    def phase_r():
        for h in hs:

            @pl.when(idx < n - 1)
            def _():
                r_copy(h).wait_recv()

            @pl.when((idx > 0) & (idx < n - 1))
            def _():
                d_out[h] = nt3(split(d_in[h]), trans[h]) + back[h]
                r_copy(h).start()

        for h in hs:
            g_full = g0[h] + nn3(split(d_in[h]), z_t[h])
            gt_s[h] = g_full
            e_t = g_full * b_row[h]
            gv_ref[base + h] = e_t[:half]
            gvx[h] = e_t[half:]
            gv_copy(h).start()

    pl.when(2 * idx < n)(phase_f)
    phase_r()
    pl.when(2 * idx >= n)(phase_f)

    for h in hs:
        g_full, d_t = gt_s[h], dt_s[h]
        d_tok = split(d_t.T)
        e_tok = split(-(g_full * b_row[h]).T)
        n_un = jnp.where(above, nn3(d_tok, split(g_full)), 0.0)
        gbx[sub, pl.ds(h, 1), :] = jnp.sum(g_full * xt_s[h], axis=0, keepdims=True) - jnp.sum(
            n_un * both[h], axis=0, keepdims=True
        )
        n_t = n_un * -b_row[h]
        sym = split((n_t + n_t.T) * r_row[h])
        d_unit = nn(
            left3(e_tok) + left3(d_tok) + list(sym) + list(split(dm_s[h])),
            right3(split(s_in[h])) + right3(split(d_in[h])) + [kb[h]] * 2 + [qb[h]] * 2,
        )
        unit = kf[h] * r_col[h]
        gk_ref[base + h] = r_col[h] * (
            d_unit - unit * jnp.sum(d_unit * unit, axis=1, keepdims=True)
        )
        k_copy(h).start()
    gb_copy.start()

    v_copy.wait_send()
    g_copy.wait_send()

    @pl.when(idx < n - 1)
    def _():
        for h in hs:
            f_copy(h).wait_send()

    @pl.when(idx > 0)
    def _():
        for h in hs:
            r_copy(h).wait_send()

    for h in hs:
        q_copy(h).wait()
        gv_copy(h).wait()
        k_copy(h).wait()
    gb_copy.wait()
    for s in range(2):
        gb_ref[s * mine : (s + 1) * mine, :] = gbx[s, :mine, :]


def solution(mesh):
    n = mesh.shape["seq"]

    def shards(query, key, value, beta, d_out):
        heads, toks, width = query.shape
        mine, half = heads // 2, value.shape[1]
        full = 2 * half
        vm = pl.BlockSpec(memory_space=pltpu.VMEM)
        dma = pltpu.SemaphoreType.DMA
        square = pltpu.VMEM((mine, full, width), F32)
        by_tok = pltpu.VMEM((mine, full, toks), F32)
        return pl.pallas_call(
            functools.partial(kernel, n),
            out_shape=(
                jax.ShapeDtypeStruct(query.shape, F32),
                jax.ShapeDtypeStruct(key.shape, F32),
                jax.ShapeDtypeStruct(value.shape, F32),
                jax.ShapeDtypeStruct(beta.shape, F32),
            ),
            in_specs=[vm] * 5,
            out_specs=(vm,) * 4,
            scratch_shapes=[
                pltpu.VMEM((mine, half, toks), BF16),
                pltpu.VMEM((mine, half, toks), BF16),
                square, square, square, square,
                by_tok, by_tok,
                pltpu.VMEM((mine, toks, toks), F32),
                by_tok,
                pltpu.VMEM((mine, half, toks), F32),
                pltpu.VMEM((2, 8, toks), F32),
                dma((2,)), dma((2,)),
                dma((mine,)), dma((mine,)),
                dma((mine,)), dma((mine,)),
                dma((4, mine)), dma((4, mine)),
            ],
            compiler_params=pltpu.CompilerParams(
                collective_id=0, has_side_effects=True, vmem_limit_bytes=32 * 2**20
            ),
        )(query, key, value, beta, d_out)

    rows = P("head", ("groups", "seq"), None)
    cols = P("head", "sub", ("groups", "seq"))
    flat = P("head", ("groups", "seq"))
    return jax.shard_map(
        shards,
        mesh=mesh,
        in_specs=(rows, rows, cols, flat, cols),
        out_specs=(rows, rows, cols, flat),
        check_vma=False,
    )
```

```python
import functools

import jax
import jax.numpy as jnp
from jax import lax
from jax.experimental import pallas as pl
from jax.experimental.pallas import tpu as pltpu
from jax.sharding import PartitionSpec as P

EPS = 1e-06
BASE = 16
PIECES = 2
F32 = jnp.float32
BF16 = jnp.bfloat16
MESH = pl.DeviceIdType.MESH


def split(x):
    hi = x.astype(BF16)
    return hi, (x - hi.astype(F32)).astype(BF16)


def nn(lhs, rhs):
    a = lhs[0] if len(lhs) == 1 else jnp.concatenate(lhs, axis=1)
    b = rhs[0] if len(rhs) == 1 else jnp.concatenate(rhs, axis=0)
    return jnp.dot(a, b, preferred_element_type=F32)


def nt(lhs, rhs):
    a = lhs[0] if len(lhs) == 1 else jnp.concatenate(lhs, axis=1)
    b = rhs[0] if len(rhs) == 1 else jnp.concatenate(rhs, axis=1)
    return lax.dot_general(a, b, (((1,), (1,)), ((), ())), preferred_element_type=F32)


def left3(s):
    return [s[0], s[0], s[1]]


def right3(s):
    return [s[0], s[1], s[0]]


def nn3(a, b):
    return nn(left3(a), right3(b))


def nt3(a, b):
    return nt(left3(a), right3(b))


def inverses(mats, row, col):
    size = mats[0].shape[0]
    heads = range(len(mats))
    eye = (row == col).astype(F32)
    near = (row // BASE) == (col // BASE)
    power = [split(jnp.where(near, -a, 0.0)) for a in mats]
    inv = [eye + jnp.where(near, -a, 0.0) for a in mats]
    reach = 2
    while reach < BASE:
        power = [split(nn3(p, p)) for p in power]
        inv = [inv[h] + nn3(split(inv[h]), power[h]) for h in heads]
        reach *= 2
    width = BASE
    while width < size:
        pair = ((row // (2 * width)) == (col // (2 * width))) & ((row // width) != (col // width))
        off = [split(jnp.where(pair, a, 0.0)) for a in mats]
        cut = [split(i) for i in inv]
        mid = [split(nn3(off[h], cut[h])) for h in heads]
        inv = [inv[h] - nn3(cut[h], mid[h]) for h in heads]
        width *= 2
    return inv


def kernel(
    n, q_ref, k_ref, v_ref, b_ref, g_ref, gq_ref, gk_ref, gv_ref, gb_ref,
    q_own, k_own, b_own, v_own, g_own, s_in, s_out, d_in, d_out, dt_s, xt_s, dm_s, gt_s, gvx, gbx,
    load, in_send, in_recv, f_send, f_recv, r_send, r_recv, o_send, o_recv,
):
    heads, toks, width = q_ref.shape
    mine = heads // 2
    half = v_ref.shape[1]
    idx = lax.axis_index("seq")
    sub = lax.axis_index("sub")
    other = 1 - sub
    right, left = lax.rem(idx + 1, n), lax.rem(idx + n - 1, n)
    scale = width ** (-0.5)
    base = sub * mine
    hs = range(mine)

    own = pl.ds(base, mine)
    first, second = pl.ds(0, half), pl.ds(half, half)
    loads = [
        pltpu.make_async_copy(src, dst, load.at[i])
        for i, (src, dst) in enumerate(
            (
                (k_ref.at[own], k_own),
                (b_ref, b_own),
                (q_ref.at[own], q_own),
                (v_ref.at[own], v_own.at[:, first]),
                (g_ref.at[own], g_own.at[:, first]),
            )
        )
    ]
    for copy in loads:
        copy.start()

    barrier = pltpu.get_barrier_semaphore()
    for target in ({"sub": other}, {"seq": right}, {"seq": left}):
        pl.semaphore_signal(barrier, inc=1, device_id=target, device_id_type=MESH)

    def remote(src, dst, send, recv, target):
        return pltpu.make_async_remote_copy(
            src_ref=src, dst_ref=dst, send_sem=send, recv_sem=recv,
            device_id=target, device_id_type=MESH,
        )

    away = pl.ds(other * mine, mine)
    v_copy = remote(v_ref.at[away], v_own.at[:, second], in_send.at[0], in_recv.at[0], {"sub": other})
    g_copy = remote(g_ref.at[away], g_own.at[:, second], in_send.at[1], in_recv.at[1], {"sub": other})

    piece = s_in.shape[1] // PIECES
    cuts = [slice(p * piece, (p + 1) * piece) for p in range(PIECES)]
    parts = [pl.ds(p * piece, piece) for p in range(PIECES)]

    def f_copy(h, p):
        return remote(
            s_out.at[h, parts[p]], s_in.at[h, parts[p]], f_send.at[h, p], f_recv.at[h, p],
            {"seq": right},
        )

    def r_copy(h, p):
        return remote(
            d_out.at[h, parts[p]], d_in.at[h, parts[p]], r_send.at[h, p], r_recv.at[h, p],
            {"seq": left},
        )

    def q_copy(h):
        at = gq_ref.at[base + h]
        return remote(at, at, o_send.at[0, h], o_recv.at[0, h], {"sub": other})

    def k_copy(h):
        at = gk_ref.at[base + h]
        return remote(at, at, o_send.at[1, h], o_recv.at[1, h], {"sub": other})

    def gv_copy(h):
        return remote(
            gvx.at[h], gv_ref.at[base + h], o_send.at[2, h], o_recv.at[2, h], {"sub": other}
        )

    gb_copy = remote(gbx.at[sub], gbx.at[sub], o_send.at[3, 0], o_recv.at[3, 0], {"sub": other})

    pl.semaphore_wait(barrier, 3)
    v_copy.start()
    g_copy.start()

    @pl.when(idx == 0)
    def _():
        s_in[...] = jnp.zeros_like(s_in)

    @pl.when(idx == n - 1)
    def _():
        d_in[...] = jnp.zeros_like(d_in)

    row = lax.broadcasted_iota(jnp.int32, (toks, toks), 0)
    col = lax.broadcasted_iota(jnp.int32, (toks, toks), 1)
    below, lower, above = row > col, row >= col, row < col
    eye = (row == col).astype(F32)

    loads[0].wait()
    loads[1].wait()
    kb = [k_own[h] for h in hs]
    kf = [k.astype(F32) for k in kb]
    r_col = [lax.rsqrt(jnp.sum(k * k, axis=1, keepdims=True) + EPS) for k in kf]
    r_row = [jnp.broadcast_to(r, (toks, toks)).T for r in r_col]
    b_row = [b_own[pl.ds(base + h, 1), :] for h in hs]
    b_col = [jnp.broadcast_to(b, (toks, toks)).T for b in b_row]
    both = [nt([kb[h]], [kb[h]]) * r_col[h] * r_row[h] for h in hs]
    tri = inverses([jnp.where(below, b_col[h] * both[h], 0.0) for h in hs], row, col)
    kbt = [k.T for k in kb]
    tri_b = [split(tri[h] * b_row[h]) for h in hs]
    tri_br = [split(tri[h] * (b_row[h] * r_row[h])) for h in hs]
    w_t = [nt([kbt[h]] * 2, list(tri_br[h])) for h in hs]
    trans = [split(eye - nn(list(split(w_t[h] * r_row[h])), [kb[h]] * 2)) for h in hs]
    w_s = [split(w) for w in w_t]

    for copy in loads[2:]:
        copy.wait()
    v_copy.wait_recv()
    g_copy.wait_recv()
    qb = [q_own[h] for h in hs]
    vt = [v_own[h] for h in hs]
    gt = [g_own[h] for h in hs]
    u_t = [nt([vt[h]] * 2, list(tri_b[h])) for h in hs]
    carry = [nn(list(split(u_t[h] * r_row[h])), [kb[h]] * 2) for h in hs]

    @pl.when(idx == 0)
    def _():
        for h in hs:
            s_out[h] = carry[h]
            for p in range(PIECES):
                f_copy(h, p).start()

    scores = [
        split(jnp.where(lower, nt([qb[h]], [kb[h]]) * (r_row[h] * scale), 0.0)) for h in hs
    ]
    dd0 = [split(nn([gt[h]] * 2, list(scores[h]))) for h in hs]
    tri_s = [split(t) for t in tri]
    g0 = [nn3(dd0[h], tri_s[h]) for h in hs]
    back = [
        nn([gt[h]], [qb[h]]) * scale
        - nn(list(split(g0[h] * (b_row[h] * r_row[h]))), [kb[h]] * 2)
        for h in hs
    ]

    @pl.when(idx == n - 1)
    def _():
        for h in hs:
            d_out[h] = back[h]
            for p in range(PIECES):
                r_copy(h, p).start()

    z_t = [
        split(nn([kbt[h]] * 2, list(split(tri[h] * r_col[h])))) for h in hs
    ]
    g_tok = [g.T for g in gt]

    def phase_f(h):
        for p in range(PIECES):

            @pl.when(idx > 0)
            def _():
                f_copy(h, p).wait_recv()

            @pl.when((idx > 0) & (idx < n - 1))
            def _():
                s_out[h, cuts[p]] = nn3(split(s_in[h, cuts[p]]), trans[h]) + carry[h][cuts[p]]
                f_copy(h, p).start()

        state = split(s_in[h])
        d_t = u_t[h] - nn3(state, w_s[h])
        xt_s[h] = vt[h].astype(F32) - nt(list(state), [kb[h]] * 2) * r_row[h]
        dt_s[h] = d_t
        dm = jnp.where(lower, nn([g_tok[h]] * 2, list(split(d_t))), 0.0)
        dm_s[h] = dm.T * scale
        gq_ref[base + h] = scale * nn(
            [g_tok[h]] * 2 + list(split(dm * r_row[h])), list(state) + [kb[h]] * 2
        )
        q_copy(h).start()

    def phase_r(h):
        for p in range(PIECES):

            @pl.when(idx < n - 1)
            def _():
                r_copy(h, p).wait_recv()

            @pl.when((idx > 0) & (idx < n - 1))
            def _():
                d_out[h, cuts[p]] = nt3(split(d_in[h, cuts[p]]), trans[h]) + back[h][cuts[p]]
                r_copy(h, p).start()

        g_full = g0[h] + nn3(split(d_in[h]), z_t[h])
        gt_s[h] = g_full
        e_t = g_full * b_row[h]
        gv_ref[base + h] = e_t[:half]
        gvx[h] = e_t[half:]
        gv_copy(h).start()

    def finish(h):
        g_full, d_t = gt_s[h], dt_s[h]
        d_tok = split(d_t.T)
        e_tok = split(-(g_full * b_row[h]).T)
        n_un = jnp.where(above, nn3(d_tok, split(g_full)), 0.0)
        gbx[sub, pl.ds(h, 1), :] = jnp.sum(g_full * xt_s[h], axis=0, keepdims=True) - jnp.sum(
            n_un * both[h], axis=0, keepdims=True
        )
        n_t = n_un * -b_row[h]
        sym = split((n_t + n_t.T) * r_row[h])
        d_unit = nn(
            left3(e_tok) + left3(d_tok) + list(sym) + list(split(dm_s[h])),
            right3(split(s_in[h])) + right3(split(d_in[h])) + [kb[h]] * 2 + [qb[h]] * 2,
        )
        unit = kf[h] * r_col[h]
        gk_ref[base + h] = r_col[h] * (
            d_unit - unit * jnp.sum(d_unit * unit, axis=1, keepdims=True)
        )
        k_copy(h).start()

    @pl.when(2 * idx < n)
    def _():
        for h in hs:
            phase_f(h)
        for h in hs:
            phase_r(h)
            finish(h)

    @pl.when(2 * idx >= n)
    def _():
        for h in hs:
            phase_r(h)
        for h in hs:
            phase_f(h)
            finish(h)

    gb_copy.start()

    v_copy.wait_send()
    g_copy.wait_send()

    @pl.when(idx < n - 1)
    def _():
        for h in hs:
            for p in range(PIECES):
                f_copy(h, p).wait_send()

    @pl.when(idx > 0)
    def _():
        for h in hs:
            for p in range(PIECES):
                r_copy(h, p).wait_send()

    for h in hs:
        q_copy(h).wait()
        gv_copy(h).wait()
        k_copy(h).wait()
    gb_copy.wait()
    for s in range(2):
        gb_ref[s * mine : (s + 1) * mine, :] = gbx[s, :mine, :]


def write_out(*refs):
    sems = refs[-1]
    copies = [pltpu.make_async_copy(refs[i], refs[4 + i], sems.at[i]) for i in range(4)]
    for copy in copies:
        copy.start()
    for copy in copies:
        copy.wait()


def solution(mesh):
    n = mesh.shape["seq"]

    def shards(query, key, value, beta, d_out):
        heads, toks, width = query.shape
        mine, half = heads // 2, value.shape[1]
        full = 2 * half
        vm = pl.BlockSpec(memory_space=pltpu.VMEM)
        hbm = pl.BlockSpec(memory_space=pltpu.HBM)
        dma = pltpu.SemaphoreType.DMA
        square = pltpu.VMEM((mine, full, width), F32)
        by_tok = pltpu.VMEM((mine, full, toks), F32)
        pinned = [pltpu.with_memory_space_constraint(x, pltpu.HBM) for x in (query, key, value, beta, d_out)]
        found = pl.pallas_call(
            functools.partial(kernel, n),
            out_shape=(
                pltpu.VMEM(query.shape, F32),
                pltpu.VMEM(key.shape, F32),
                pltpu.VMEM(value.shape, F32),
                pltpu.VMEM(beta.shape, F32),
            ),
            in_specs=[hbm] * 5,
            out_specs=(vm,) * 4,
            scratch_shapes=[
                pltpu.VMEM((mine, toks, width), BF16),
                pltpu.VMEM((mine, toks, width), BF16),
                pltpu.VMEM((heads, toks), F32),
                pltpu.VMEM((mine, full, toks), BF16),
                pltpu.VMEM((mine, full, toks), BF16),
                square, square, square, square,
                by_tok, by_tok,
                pltpu.VMEM((mine, toks, toks), F32),
                by_tok,
                pltpu.VMEM((mine, half, toks), F32),
                pltpu.VMEM((2, 8, toks), F32),
                dma((5,)), dma((2,)), dma((2,)),
                dma((mine, PIECES)), dma((mine, PIECES)),
                dma((mine, PIECES)), dma((mine, PIECES)),
                dma((4, mine)), dma((4, mine)),
            ],
            compiler_params=pltpu.CompilerParams(
                collective_id=0, has_side_effects=True, vmem_limit_bytes=32 * 2**20
            ),
        )(*pinned)
        return pl.pallas_call(
            write_out,
            out_shape=tuple(jax.ShapeDtypeStruct(x.shape, F32) for x in found),
            in_specs=[vm] * 4,
            out_specs=(hbm,) * 4,
            scratch_shapes=[dma((4,))],
        )(*[pltpu.with_memory_space_constraint(x, pltpu.VMEM) for x in found])

    rows = P("head", ("groups", "seq"), None)
    cols = P("head", "sub", ("groups", "seq"))
    flat = P("head", ("groups", "seq"))
    return jax.shard_map(
        shards,
        mesh=mesh,
        in_specs=(rows, rows, cols, flat, cols),
        out_specs=(rows, rows, cols, flat),
        check_vma=False,
    )
```

```python
import functools

import jax
import jax.numpy as jnp
from jax import lax
from jax.experimental import pallas as pl
from jax.experimental.pallas import tpu as pltpu
from jax.sharding import PartitionSpec as P

EPS = 1e-06
BASE = 32
PIECES = 2
F32 = jnp.float32
BF16 = jnp.bfloat16
MESH = pl.DeviceIdType.MESH


def split(x):
    hi = x.astype(BF16)
    return hi, (x - hi.astype(F32)).astype(BF16)


def nn(lhs, rhs):
    a = lhs[0] if len(lhs) == 1 else jnp.concatenate(lhs, axis=1)
    b = rhs[0] if len(rhs) == 1 else jnp.concatenate(rhs, axis=0)
    return jnp.dot(a, b, preferred_element_type=F32)


def nt(lhs, rhs):
    a = lhs[0] if len(lhs) == 1 else jnp.concatenate(lhs, axis=1)
    b = rhs[0] if len(rhs) == 1 else jnp.concatenate(rhs, axis=1)
    return lax.dot_general(a, b, (((1,), (1,)), ((), ())), preferred_element_type=F32)


def left3(s):
    return [s[0], s[0], s[1]]


def right3(s):
    return [s[0], s[1], s[0]]


def nn3(a, b):
    return nn(left3(a), right3(b))


def nt3(a, b):
    return nt(left3(a), right3(b))


def inverses(mats, row, col):
    size = mats[0].shape[0]
    heads = range(len(mats))
    eye = (row == col).astype(F32)
    near = (row // BASE) == (col // BASE)
    power = [split(jnp.where(near, -a, 0.0)) for a in mats]
    inv = [eye + jnp.where(near, -a, 0.0) for a in mats]
    reach = 2
    while reach < BASE:
        power = [split(nn3(p, p)) for p in power]
        inv = [inv[h] + nn3(split(inv[h]), power[h]) for h in heads]
        reach *= 2
    width = BASE
    while width < size:
        pair = ((row // (2 * width)) == (col // (2 * width))) & ((row // width) != (col // width))
        off = [split(jnp.where(pair, a, 0.0)) for a in mats]
        cut = [split(i) for i in inv]
        mid = [split(nn3(off[h], cut[h])) for h in heads]
        inv = [inv[h] - nn3(cut[h], mid[h]) for h in heads]
        width *= 2
    return inv


def kernel(
    n, q_ref, k_ref, v_ref, b_ref, g_ref, gq_ref, gk_ref, gv_ref, gb_ref,
    q_own, k_own, b_own, v_own, g_own, s_in, s_out, d_in, d_out, dt_s, xt_s, dm_s, gt_s, gvx, gbx,
    load, in_send, in_recv, f_send, f_recv, r_send, r_recv, o_send, o_recv,
):
    heads, toks, width = q_ref.shape
    mine = heads // 2
    half = v_ref.shape[1]
    idx = lax.axis_index("seq")
    sub = lax.axis_index("sub")
    other = 1 - sub
    right, left = lax.rem(idx + 1, n), lax.rem(idx + n - 1, n)
    scale = width ** (-0.5)
    base = sub * mine
    hs = range(mine)

    own = pl.ds(base, mine)
    first, second = pl.ds(0, half), pl.ds(half, half)
    loads = [
        pltpu.make_async_copy(src, dst, load.at[i])
        for i, (src, dst) in enumerate(
            (
                (k_ref.at[own], k_own),
                (b_ref, b_own),
                (q_ref.at[own], q_own),
                (v_ref.at[own], v_own.at[:, first]),
                (g_ref.at[own], g_own.at[:, first]),
            )
        )
    ]
    for copy in loads:
        copy.start()

    barrier = pltpu.get_barrier_semaphore()
    for target in ({"sub": other}, {"seq": right}, {"seq": left}):
        pl.semaphore_signal(barrier, inc=1, device_id=target, device_id_type=MESH)

    def remote(src, dst, send, recv, target):
        return pltpu.make_async_remote_copy(
            src_ref=src, dst_ref=dst, send_sem=send, recv_sem=recv,
            device_id=target, device_id_type=MESH,
        )

    away = pl.ds(other * mine, mine)
    v_copy = remote(v_ref.at[away], v_own.at[:, second], in_send.at[0], in_recv.at[0], {"sub": other})
    g_copy = remote(g_ref.at[away], g_own.at[:, second], in_send.at[1], in_recv.at[1], {"sub": other})

    piece = s_in.shape[1] // PIECES
    cuts = [slice(p * piece, (p + 1) * piece) for p in range(PIECES)]
    parts = [pl.ds(p * piece, piece) for p in range(PIECES)]

    def f_copy(h, p):
        return remote(
            s_out.at[h, parts[p]], s_in.at[h, parts[p]], f_send.at[h, p], f_recv.at[h, p],
            {"seq": right},
        )

    def r_copy(h, p):
        return remote(
            d_out.at[h, parts[p]], d_in.at[h, parts[p]], r_send.at[h, p], r_recv.at[h, p],
            {"seq": left},
        )

    def q_copy(h):
        at = gq_ref.at[base + h]
        return remote(at, at, o_send.at[0, h], o_recv.at[0, h], {"sub": other})

    def k_copy(h):
        at = gk_ref.at[base + h]
        return remote(at, at, o_send.at[1, h], o_recv.at[1, h], {"sub": other})

    def gv_copy(h):
        return remote(
            gvx.at[h], gv_ref.at[base + h], o_send.at[2, h], o_recv.at[2, h], {"sub": other}
        )

    gb_copy = remote(gbx.at[sub], gbx.at[sub], o_send.at[3, 0], o_recv.at[3, 0], {"sub": other})

    pl.semaphore_wait(barrier, 3)
    v_copy.start()
    g_copy.start()

    @pl.when(idx == 0)
    def _():
        s_in[...] = jnp.zeros_like(s_in)

    @pl.when(idx == n - 1)
    def _():
        d_in[...] = jnp.zeros_like(d_in)

    row = lax.broadcasted_iota(jnp.int32, (toks, toks), 0)
    col = lax.broadcasted_iota(jnp.int32, (toks, toks), 1)
    below, lower, above = row > col, row >= col, row < col
    eye = (row == col).astype(F32)

    loads[0].wait()
    loads[1].wait()
    kb = [k_own[h] for h in hs]
    kf = [k.astype(F32) for k in kb]
    r_col = [lax.rsqrt(jnp.sum(k * k, axis=1, keepdims=True) + EPS) for k in kf]
    r_row = [jnp.broadcast_to(r, (toks, toks)).T for r in r_col]
    b_row = [b_own[pl.ds(base + h, 1), :] for h in hs]
    b_col = [jnp.broadcast_to(b, (toks, toks)).T for b in b_row]
    both = [nt([kb[h]], [kb[h]]) * r_col[h] * r_row[h] for h in hs]
    tri = inverses([jnp.where(below, b_col[h] * both[h], 0.0) for h in hs], row, col)
    kbt = [k.T for k in kb]
    tri_b = [split(tri[h] * b_row[h]) for h in hs]
    tri_br = [split(tri[h] * (b_row[h] * r_row[h])) for h in hs]
    w_t = [nt([kbt[h]] * 2, list(tri_br[h])) for h in hs]
    trans = [split(eye - nn(list(split(w_t[h] * r_row[h])), [kb[h]] * 2)) for h in hs]
    w_s = [split(w) for w in w_t]

    for copy in loads[2:]:
        copy.wait()
    v_copy.wait_recv()
    g_copy.wait_recv()
    qb = [q_own[h] for h in hs]
    vt = [v_own[h] for h in hs]
    gt = [g_own[h] for h in hs]
    u_t = [nt([vt[h]] * 2, list(tri_b[h])) for h in hs]
    carry = [nn(list(split(u_t[h] * r_row[h])), [kb[h]] * 2) for h in hs]

    @pl.when(idx == 0)
    def _():
        for h in hs:
            s_out[h] = carry[h]
            for p in range(PIECES):
                f_copy(h, p).start()

    scores = [
        split(jnp.where(lower, nt([qb[h]], [kb[h]]) * (r_row[h] * scale), 0.0)) for h in hs
    ]
    dd0 = [split(nn([gt[h]] * 2, list(scores[h]))) for h in hs]
    tri_s = [split(t) for t in tri]
    g0 = [nn3(dd0[h], tri_s[h]) for h in hs]
    back = [
        nn([gt[h]], [qb[h]]) * scale
        - nn(list(split(g0[h] * (b_row[h] * r_row[h]))), [kb[h]] * 2)
        for h in hs
    ]

    @pl.when(idx == n - 1)
    def _():
        for h in hs:
            d_out[h] = back[h]
            for p in range(PIECES):
                r_copy(h, p).start()

    z_t = [
        split(nn([kbt[h]] * 2, list(split(tri[h] * r_col[h])))) for h in hs
    ]
    g_tok = [g.T for g in gt]

    inside = (idx > 0) & (idx < n - 1)

    def relay_f():
        @pl.when(inside)
        def _():
            for h in hs:
                for p in range(PIECES):
                    f_copy(h, p).wait_recv()
                    s_out[h, cuts[p]] = nn3(split(s_in[h, cuts[p]]), trans[h]) + carry[h][cuts[p]]
                    f_copy(h, p).start()

    def relay_r():
        @pl.when(inside)
        def _():
            for h in hs:
                for p in range(PIECES):
                    r_copy(h, p).wait_recv()
                    d_out[h, cuts[p]] = nt3(split(d_in[h, cuts[p]]), trans[h]) + back[h][cuts[p]]
                    r_copy(h, p).start()

    def phase_f(h):
        @pl.when(idx == n - 1)
        def _():
            for p in range(PIECES):
                f_copy(h, p).wait_recv()

        state = split(s_in[h])
        d_t = u_t[h] - nn3(state, w_s[h])
        xt_s[h] = vt[h].astype(F32) - nt(list(state), [kb[h]] * 2) * r_row[h]
        dt_s[h] = d_t
        dm = jnp.where(lower, nn([g_tok[h]] * 2, list(split(d_t))), 0.0)
        dm_s[h] = dm.T * scale
        gq_ref[base + h] = scale * nn(
            [g_tok[h]] * 2 + list(split(dm * r_row[h])), list(state) + [kb[h]] * 2
        )
        q_copy(h).start()

    def phase_r(h):
        @pl.when(idx == 0)
        def _():
            for p in range(PIECES):
                r_copy(h, p).wait_recv()

        g_full = g0[h] + nn3(split(d_in[h]), z_t[h])
        gt_s[h] = g_full
        e_t = g_full * b_row[h]
        gv_ref[base + h] = e_t[:half]
        gvx[h] = e_t[half:]
        gv_copy(h).start()

    def finish(h):
        g_full, d_t = gt_s[h], dt_s[h]
        d_tok = split(d_t.T)
        e_tok = split(-(g_full * b_row[h]).T)
        n_un = jnp.where(above, nn3(d_tok, split(g_full)), 0.0)
        gbx[sub, pl.ds(h, 1), :] = jnp.sum(g_full * xt_s[h], axis=0, keepdims=True) - jnp.sum(
            n_un * both[h], axis=0, keepdims=True
        )
        n_t = n_un * -b_row[h]
        sym = split((n_t + n_t.T) * r_row[h])
        d_unit = nn(
            left3(e_tok) + left3(d_tok) + list(sym) + list(split(dm_s[h])),
            right3(split(s_in[h])) + right3(split(d_in[h])) + [kb[h]] * 2 + [qb[h]] * 2,
        )
        unit = kf[h] * r_col[h]
        gk_ref[base + h] = r_col[h] * (
            d_unit - unit * jnp.sum(d_unit * unit, axis=1, keepdims=True)
        )
        k_copy(h).start()

    @pl.when(2 * idx < n)
    def _():
        relay_f()
        for h in hs:
            phase_f(h)
        relay_r()
        for h in hs:
            phase_r(h)
            finish(h)

    @pl.when(2 * idx >= n)
    def _():
        relay_r()
        for h in hs:
            phase_r(h)
        relay_f()
        for h in hs:
            phase_f(h)
            finish(h)

    gb_copy.start()

    v_copy.wait_send()
    g_copy.wait_send()

    @pl.when(idx < n - 1)
    def _():
        for h in hs:
            for p in range(PIECES):
                f_copy(h, p).wait_send()

    @pl.when(idx > 0)
    def _():
        for h in hs:
            for p in range(PIECES):
                r_copy(h, p).wait_send()

    for h in hs:
        q_copy(h).wait()
        gv_copy(h).wait()
        k_copy(h).wait()
    gb_copy.wait()
    for s in range(2):
        gb_ref[s * mine : (s + 1) * mine, :] = gbx[s, :mine, :]


def write_out(*refs):
    sems = refs[-1]
    copies = [pltpu.make_async_copy(refs[i], refs[4 + i], sems.at[i]) for i in range(4)]
    for copy in copies:
        copy.start()
    for copy in copies:
        copy.wait()


def solution(mesh):
    n = mesh.shape["seq"]

    def shards(query, key, value, beta, d_out):
        heads, toks, width = query.shape
        mine, half = heads // 2, value.shape[1]
        full = 2 * half
        vm = pl.BlockSpec(memory_space=pltpu.VMEM)
        hbm = pl.BlockSpec(memory_space=pltpu.HBM)
        dma = pltpu.SemaphoreType.DMA
        square = pltpu.VMEM((mine, full, width), F32)
        by_tok = pltpu.VMEM((mine, full, toks), F32)
        pinned = [pltpu.with_memory_space_constraint(x, pltpu.HBM) for x in (query, key, value, beta, d_out)]
        found = pl.pallas_call(
            functools.partial(kernel, n),
            out_shape=(
                pltpu.VMEM(query.shape, F32),
                pltpu.VMEM(key.shape, F32),
                pltpu.VMEM(value.shape, F32),
                pltpu.VMEM(beta.shape, F32),
            ),
            in_specs=[hbm] * 5,
            out_specs=(vm,) * 4,
            scratch_shapes=[
                pltpu.VMEM((mine, toks, width), BF16),
                pltpu.VMEM((mine, toks, width), BF16),
                pltpu.VMEM((heads, toks), F32),
                pltpu.VMEM((mine, full, toks), BF16),
                pltpu.VMEM((mine, full, toks), BF16),
                square, square, square, square,
                by_tok, by_tok,
                pltpu.VMEM((mine, toks, toks), F32),
                by_tok,
                pltpu.VMEM((mine, half, toks), F32),
                pltpu.VMEM((2, 8, toks), F32),
                dma((5,)), dma((2,)), dma((2,)),
                dma((mine, PIECES)), dma((mine, PIECES)),
                dma((mine, PIECES)), dma((mine, PIECES)),
                dma((4, mine)), dma((4, mine)),
            ],
            compiler_params=pltpu.CompilerParams(
                collective_id=0, has_side_effects=True, vmem_limit_bytes=32 * 2**20
            ),
        )(*pinned)
        return pl.pallas_call(
            write_out,
            out_shape=tuple(jax.ShapeDtypeStruct(x.shape, F32) for x in found),
            in_specs=[vm] * 4,
            out_specs=(hbm,) * 4,
            scratch_shapes=[dma((4,))],
        )(*[pltpu.with_memory_space_constraint(x, pltpu.VMEM) for x in found])

    rows = P("head", ("groups", "seq"), None)
    cols = P("head", "sub", ("groups", "seq"))
    flat = P("head", ("groups", "seq"))
    return jax.shard_map(
        shards,
        mesh=mesh,
        in_specs=(rows, rows, cols, flat, cols),
        out_specs=(rows, rows, cols, flat),
        check_vma=False,
    )
```

```python
import functools

import jax
import jax.numpy as jnp
from jax import lax
from jax.experimental import pallas as pl
from jax.experimental.pallas import tpu as pltpu
from jax.sharding import PartitionSpec as P

EPS = 1e-06
BASE = 32
PIECES = 2
F32 = jnp.float32
BF16 = jnp.bfloat16
MESH = pl.DeviceIdType.MESH


def split(x):
    hi = x.astype(BF16)
    return hi, (x - hi.astype(F32)).astype(BF16)


def nn(lhs, rhs):
    a = lhs[0] if len(lhs) == 1 else jnp.concatenate(lhs, axis=1)
    b = rhs[0] if len(rhs) == 1 else jnp.concatenate(rhs, axis=0)
    return jnp.dot(a, b, preferred_element_type=F32)


def nt(lhs, rhs):
    a = lhs[0] if len(lhs) == 1 else jnp.concatenate(lhs, axis=1)
    b = rhs[0] if len(rhs) == 1 else jnp.concatenate(rhs, axis=1)
    return lax.dot_general(a, b, (((1,), (1,)), ((), ())), preferred_element_type=F32)


def left3(s):
    return [s[0], s[0], s[1]]


def right3(s):
    return [s[0], s[1], s[0]]


def nn3(a, b):
    return nn(left3(a), right3(b))


def nt3(a, b):
    return nt(left3(a), right3(b))


def inverses(mats, row, col):
    size = mats[0].shape[0]
    heads = range(len(mats))
    eye = (row == col).astype(F32)
    near = (row // BASE) == (col // BASE)
    power = [split(jnp.where(near, -a, 0.0)) for a in mats]
    inv = [eye + jnp.where(near, -a, 0.0) for a in mats]
    reach = 2
    while reach < BASE:
        power = [split(nn3(p, p)) for p in power]
        inv = [inv[h] + nn3(split(inv[h]), power[h]) for h in heads]
        reach *= 2
    width = BASE
    while width < size:
        pair = ((row // (2 * width)) == (col // (2 * width))) & ((row // width) != (col // width))
        off = [split(jnp.where(pair, a, 0.0)) for a in mats]
        cut = [split(i) for i in inv]
        mid = [split(nn3(off[h], cut[h])) for h in heads]
        inv = [inv[h] - nn3(cut[h], mid[h]) for h in heads]
        width *= 2
    return inv


def kernel(
    n, q_ref, k_ref, v_ref, b_ref, g_ref, gq_ref, gk_ref, gv_ref, gb_ref,
    q_own, k_own, b_own, v_own, g_own, s_in, s_out, d_in, d_out, dt_s, xt_s, dm_s, gt_s, gvx, gbx,
    load, in_send, in_recv, f_send, f_recv, r_send, r_recv, o_send, o_recv,
):
    heads, toks, width = q_ref.shape
    mine = heads // 2
    half = v_ref.shape[1]
    idx = lax.axis_index("seq")
    sub = lax.axis_index("sub")
    other = 1 - sub
    right, left = lax.rem(idx + 1, n), lax.rem(idx + n - 1, n)
    scale = width ** (-0.5)
    base = sub * mine
    hs = range(mine)

    own = pl.ds(base, mine)
    first, second = pl.ds(0, half), pl.ds(half, half)
    loads = [
        pltpu.make_async_copy(src, dst, load.at[i])
        for i, (src, dst) in enumerate(
            (
                (k_ref.at[own], k_own),
                (b_ref, b_own),
                (q_ref.at[own], q_own),
                (v_ref.at[own], v_own.at[:, first]),
                (g_ref.at[own], g_own.at[:, first]),
            )
        )
    ]
    for copy in loads:
        copy.start()

    barrier = pltpu.get_barrier_semaphore()
    inside = (idx > 0) & (idx < n - 1)

    def greet(target):
        pl.semaphore_signal(barrier, inc=1, device_id=target, device_id_type=MESH)

    greet({"sub": other})

    @pl.when(idx < n - 1)
    def _():
        greet({"seq": right})

    @pl.when(idx > 0)
    def _():
        greet({"seq": left})

    def remote(src, dst, send, recv, target):
        return pltpu.make_async_remote_copy(
            src_ref=src, dst_ref=dst, send_sem=send, recv_sem=recv,
            device_id=target, device_id_type=MESH,
        )

    away = pl.ds(other * mine, mine)
    v_copy = remote(v_ref.at[away], v_own.at[:, second], in_send.at[0], in_recv.at[0], {"sub": other})
    g_copy = remote(g_ref.at[away], g_own.at[:, second], in_send.at[1], in_recv.at[1], {"sub": other})

    piece = s_in.shape[1] // PIECES
    cuts = [slice(p * piece, (p + 1) * piece) for p in range(PIECES)]
    parts = [pl.ds(p * piece, piece) for p in range(PIECES)]

    def f_copy(h, p):
        return remote(
            s_out.at[h, parts[p]], s_in.at[h, parts[p]], f_send.at[h, p], f_recv.at[h, p],
            {"seq": right},
        )

    def r_copy(h, p):
        return remote(
            d_out.at[h, parts[p]], d_in.at[h, parts[p]], r_send.at[h, p], r_recv.at[h, p],
            {"seq": left},
        )

    def q_copy(h):
        at = gq_ref.at[base + h]
        return remote(at, at, o_send.at[0, h], o_recv.at[0, h], {"sub": other})

    def k_copy(h):
        at = gk_ref.at[base + h]
        return remote(at, at, o_send.at[1, h], o_recv.at[1, h], {"sub": other})

    def gv_copy(h):
        return remote(
            gvx.at[h], gv_ref.at[base + h], o_send.at[2, h], o_recv.at[2, h], {"sub": other}
        )

    gb_copy = remote(gbx.at[sub], gbx.at[sub], o_send.at[3, 0], o_recv.at[3, 0], {"sub": other})

    @pl.when(inside)
    def _():
        pl.semaphore_wait(barrier, 3)

    @pl.when(jnp.logical_not(inside))
    def _():
        pl.semaphore_wait(barrier, 2)

    v_copy.start()
    g_copy.start()

    @pl.when(idx == 0)
    def _():
        s_in[...] = jnp.zeros_like(s_in)

    @pl.when(idx == n - 1)
    def _():
        d_in[...] = jnp.zeros_like(d_in)

    row = lax.broadcasted_iota(jnp.int32, (toks, toks), 0)
    col = lax.broadcasted_iota(jnp.int32, (toks, toks), 1)
    below, lower, above = row > col, row >= col, row < col
    eye = (row == col).astype(F32)

    loads[0].wait()
    loads[1].wait()
    kb = [k_own[h] for h in hs]
    kf = [k.astype(F32) for k in kb]
    r_col = [lax.rsqrt(jnp.sum(k * k, axis=1, keepdims=True) + EPS) for k in kf]
    r_row = [jnp.broadcast_to(r, (toks, toks)).T for r in r_col]
    b_row = [b_own[pl.ds(base + h, 1), :] for h in hs]
    b_col = [jnp.broadcast_to(b, (toks, toks)).T for b in b_row]
    both = [nt([kb[h]], [kb[h]]) * r_col[h] * r_row[h] for h in hs]
    tri = inverses([jnp.where(below, b_col[h] * both[h], 0.0) for h in hs], row, col)
    kbt = [k.T for k in kb]
    tri_b = [split(tri[h] * b_row[h]) for h in hs]
    tri_br = [split(tri[h] * (b_row[h] * r_row[h])) for h in hs]
    w_t = [nt([kbt[h]] * 2, list(tri_br[h])) for h in hs]
    trans = [split(eye - nn(list(split(w_t[h] * r_row[h])), [kb[h]] * 2)) for h in hs]
    w_s = [split(w) for w in w_t]

    for copy in loads[2:]:
        copy.wait()
    v_copy.wait_recv()
    g_copy.wait_recv()
    qb = [q_own[h] for h in hs]
    vt = [v_own[h] for h in hs]
    gt = [g_own[h] for h in hs]
    u_t = [nt([vt[h]] * 2, list(tri_b[h])) for h in hs]
    carry = [nn(list(split(u_t[h] * r_row[h])), [kb[h]] * 2) for h in hs]

    @pl.when(idx == 0)
    def _():
        for h in hs:
            s_out[h] = carry[h]
            for p in range(PIECES):
                f_copy(h, p).start()

    scores = [
        split(jnp.where(lower, nt([qb[h]], [kb[h]]) * (r_row[h] * scale), 0.0)) for h in hs
    ]
    dd0 = [split(nn([gt[h]] * 2, list(scores[h]))) for h in hs]
    tri_s = [split(t) for t in tri]
    g0 = [nn3(dd0[h], tri_s[h]) for h in hs]
    back = [
        nn([gt[h]], [qb[h]]) * scale
        - nn(list(split(g0[h] * (b_row[h] * r_row[h]))), [kb[h]] * 2)
        for h in hs
    ]

    @pl.when(idx == n - 1)
    def _():
        for h in hs:
            d_out[h] = back[h]
            for p in range(PIECES):
                r_copy(h, p).start()

    z_t = [
        split(nn([kbt[h]] * 2, list(split(tri[h] * r_col[h])))) for h in hs
    ]
    g_tok = [g.T for g in gt]

    def relay_f():
        @pl.when(inside)
        def _():
            for h in hs:
                for p in range(PIECES):
                    f_copy(h, p).wait_recv()
                    s_out[h, cuts[p]] = nn3(split(s_in[h, cuts[p]]), trans[h]) + carry[h][cuts[p]]
                    f_copy(h, p).start()

    def relay_r():
        @pl.when(inside)
        def _():
            for h in hs:
                for p in range(PIECES):
                    r_copy(h, p).wait_recv()
                    d_out[h, cuts[p]] = nt3(split(d_in[h, cuts[p]]), trans[h]) + back[h][cuts[p]]
                    r_copy(h, p).start()

    def phase_f(h):
        @pl.when(idx == n - 1)
        def _():
            for p in range(PIECES):
                f_copy(h, p).wait_recv()

        state = split(s_in[h])
        d_t = u_t[h] - nn3(state, w_s[h])
        xt_s[h] = vt[h].astype(F32) - nt(list(state), [kb[h]] * 2) * r_row[h]
        dt_s[h] = d_t
        dm = jnp.where(lower, nn([g_tok[h]] * 2, list(split(d_t))), 0.0)
        dm_s[h] = dm.T * scale
        gq_ref[base + h] = scale * nn(
            [g_tok[h]] * 2 + list(split(dm * r_row[h])), list(state) + [kb[h]] * 2
        )
        q_copy(h).start()

    def phase_r(h):
        @pl.when(idx == 0)
        def _():
            for p in range(PIECES):
                r_copy(h, p).wait_recv()

        g_full = g0[h] + nn3(split(d_in[h]), z_t[h])
        gt_s[h] = g_full
        e_t = g_full * b_row[h]
        gv_ref[base + h] = e_t[:half]
        gvx[h] = e_t[half:]
        gv_copy(h).start()

    def finish(h):
        g_full, d_t = gt_s[h], dt_s[h]
        d_tok = split(d_t.T)
        e_tok = split(-(g_full * b_row[h]).T)
        n_un = jnp.where(above, nn3(d_tok, split(g_full)), 0.0)
        gbx[sub, pl.ds(h, 1), :] = jnp.sum(g_full * xt_s[h], axis=0, keepdims=True) - jnp.sum(
            n_un * both[h], axis=0, keepdims=True
        )
        n_t = n_un * -b_row[h]
        sym = split((n_t + n_t.T) * r_row[h])
        d_unit = nn(
            left3(e_tok) + left3(d_tok) + list(sym) + list(split(dm_s[h])),
            right3(split(s_in[h])) + right3(split(d_in[h])) + [kb[h]] * 2 + [qb[h]] * 2,
        )
        unit = kf[h] * r_col[h]
        gk_ref[base + h] = r_col[h] * (
            d_unit - unit * jnp.sum(d_unit * unit, axis=1, keepdims=True)
        )
        k_copy(h).start()

    @pl.when(2 * idx < n)
    def _():
        relay_f()
        for h in hs:
            phase_f(h)
        relay_r()
        for h in hs:
            phase_r(h)
            finish(h)

    @pl.when(2 * idx >= n)
    def _():
        relay_r()
        for h in hs:
            phase_r(h)
        relay_f()
        for h in hs:
            phase_f(h)
            finish(h)

    gb_copy.start()

    v_copy.wait_send()
    g_copy.wait_send()

    @pl.when(idx < n - 1)
    def _():
        for h in hs:
            for p in range(PIECES):
                f_copy(h, p).wait_send()

    @pl.when(idx > 0)
    def _():
        for h in hs:
            for p in range(PIECES):
                r_copy(h, p).wait_send()

    for h in hs:
        q_copy(h).wait()
        gv_copy(h).wait()
        k_copy(h).wait()
    gb_copy.wait()
    for s in range(2):
        gb_ref[s * mine : (s + 1) * mine, :] = gbx[s, :mine, :]


def write_out(*refs):
    sems = refs[-1]
    copies = [pltpu.make_async_copy(refs[i], refs[4 + i], sems.at[i]) for i in range(4)]
    for copy in copies:
        copy.start()
    for copy in copies:
        copy.wait()


def solution(mesh):
    n = mesh.shape["seq"]

    def shards(query, key, value, beta, d_out):
        heads, toks, width = query.shape
        mine, half = heads // 2, value.shape[1]
        full = 2 * half
        vm = pl.BlockSpec(memory_space=pltpu.VMEM)
        hbm = pl.BlockSpec(memory_space=pltpu.HBM)
        dma = pltpu.SemaphoreType.DMA
        square = pltpu.VMEM((mine, full, width), F32)
        by_tok = pltpu.VMEM((mine, full, toks), F32)
        pinned = [pltpu.with_memory_space_constraint(x, pltpu.HBM) for x in (query, key, value, beta, d_out)]
        found = pl.pallas_call(
            functools.partial(kernel, n),
            out_shape=(
                pltpu.VMEM(query.shape, F32),
                pltpu.VMEM(key.shape, F32),
                pltpu.VMEM(value.shape, F32),
                pltpu.VMEM(beta.shape, F32),
            ),
            in_specs=[hbm] * 5,
            out_specs=(vm,) * 4,
            scratch_shapes=[
                pltpu.VMEM((mine, toks, width), BF16),
                pltpu.VMEM((mine, toks, width), BF16),
                pltpu.VMEM((heads, toks), F32),
                pltpu.VMEM((mine, full, toks), BF16),
                pltpu.VMEM((mine, full, toks), BF16),
                square, square, square, square,
                by_tok, by_tok,
                pltpu.VMEM((mine, toks, toks), F32),
                by_tok,
                pltpu.VMEM((mine, half, toks), F32),
                pltpu.VMEM((2, 8, toks), F32),
                dma((5,)), dma((2,)), dma((2,)),
                dma((mine, PIECES)), dma((mine, PIECES)),
                dma((mine, PIECES)), dma((mine, PIECES)),
                dma((4, mine)), dma((4, mine)),
            ],
            compiler_params=pltpu.CompilerParams(
                collective_id=0, has_side_effects=True, vmem_limit_bytes=32 * 2**20
            ),
        )(*pinned)
        return pl.pallas_call(
            write_out,
            out_shape=tuple(jax.ShapeDtypeStruct(x.shape, F32) for x in found),
            in_specs=[vm] * 4,
            out_specs=(hbm,) * 4,
            scratch_shapes=[dma((4,))],
        )(*[pltpu.with_memory_space_constraint(x, pltpu.VMEM) for x in found])

    rows = P("head", ("groups", "seq"), None)
    cols = P("head", "sub", ("groups", "seq"))
    flat = P("head", ("groups", "seq"))
    return jax.shard_map(
        shards,
        mesh=mesh,
        in_specs=(rows, rows, cols, flat, cols),
        out_specs=(rows, rows, cols, flat),
        check_vma=False,
    )
```
